32 devices in a mesh: groups: 2 (over y), block: 4 (over z), scen: 2 (over x), dp: 2 (over core).
Axes of the slice: x: 2, y: 2, z: 4, core: 2. Of those that a mesh axis runs over, the one named last changes fastest.
Arguments:
- grad_parts: bfloat16 [2, 4, 8, 512, 512], P('dp', ('groups', 'scen'), None, 'block'), parts along dimension 1, may hold values from -16 to 16
- live_counts: int32 [4], P('groups'), parts along dimension 0, may hold values from 1 to 6, as said below
Outputs:
- direction: bfloat16 [4, 8, 512, 512], P(('groups', 'scen'), None, ('block', 'dp')), parts along dimension 0
The draws below stay inside these ranges and needn't reach their ends.
There are 2 independent parts, one for each index of `groups`. The reference program is written for one: setup_inputs(seed, part) draws one part's arguments, and reference() takes and returns one part's arrays. A program takes and returns all parts, laid end to end along the dimension named above; each array names one. Nothing has to cross between parts.
Inputs may be any that keep to these rules, and one draw needn't show every extreme that they name: `live_counts`: exactly one tower has 6 live slots; every other tower has at most 2, so the counts of all towers sum to at most 8.
All inputs are finite; a program needn't handle non-finite values.
Results may differ from the reference program's by a relative error of at most 0.001.
The reference program's roundings to bfloat16 on the way (of `summed` and `inner_rows`) count: a program that leaves them out, or rounds other values in their place, can miss the bound.
Values may be sent and summed in bfloat16 or wider, within the bound.
A program may use at most 64 MiB of HBM per device.

```python
import jax
import jax.numpy as jnp
from jax import lax

B = 512
ITERS = 2
NBLK = 8
TOWERS = 2
PAIRS = 2
LIVE_MOST = 6


def draw_grad_parts(key, part):
    key = jax.random.fold_in(key, 7)
    subkeys = jax.random.split(key, 1)
    full_shape = (PAIRS, TOWERS, NBLK, B, B)
    values = jnp.clip(jax.random.normal(subkeys[0], full_shape, jnp.float32), -6.0, 6.0)
    return values.astype(jnp.bfloat16)


def draw_live_counts(key, part):
    key = jax.random.fold_in(key, 11)
    others = jax.random.randint(key, (TOWERS,), 1, NBLK // 4 + 1, dtype=jnp.int32)
    fullest = jnp.mod(jnp.asarray(part, jnp.int32), TOWERS)
    tower_ids = jnp.arange(TOWERS, dtype=jnp.int32)
    return jnp.where(tower_ids == fullest, LIVE_MOST, others).astype(jnp.int32)


def setup_inputs(seed: int = 0, part: int = 0) -> dict:
    seeds = jax.random.split(jax.random.key(seed), 3)
    part_keys = jax.random.split(jax.random.fold_in(seeds[2], part), 3)
    return {
        "grad_parts": draw_grad_parts(jax.random.fold_in(jax.random.fold_in(seeds[2], part), 71), part),
        "live_counts": draw_live_counts(jax.random.fold_in(jax.random.fold_in(seeds[2], part), 71), part),
    }


DAMPING = 0.25
EPSILON = 1e-06
HIGHEST = lax.Precision.HIGHEST

def newton_root(statistics):
    extent = statistics.shape[0]
    identity = jnp.eye(extent, dtype=jnp.float32)
    damped = statistics + (DAMPING * jnp.trace(statistics) / extent + EPSILON) * identity
    scaled = damped / (2.0 * jnp.trace(damped) / extent)
    inverse = identity
    for iteration in range(ITERS):
        factor = (5.0 * identity - scaled) * 0.25
        if iteration == 0:
            inverse = factor
        else:
            inverse = jnp.dot(inverse, factor, precision=HIGHEST, preferred_element_type=jnp.float32)
        if iteration + 1 < ITERS:
            square = jnp.dot(factor, factor, precision=HIGHEST, preferred_element_type=jnp.float32)
            fourth = jnp.dot(square, square, precision=HIGHEST, preferred_element_type=jnp.float32)
            scaled = jnp.dot(fourth, scaled, precision=HIGHEST, preferred_element_type=jnp.float32)
    return inverse.astype(jnp.bfloat16)

def refresh(element):
    gradient, live_flag = element
    left = jnp.dot(gradient, gradient.T, preferred_element_type=jnp.float32)
    right = jnp.dot(gradient.T, gradient, preferred_element_type=jnp.float32)
    root_left = newton_root(left)
    root_right = newton_root(right)
    inner_rows = jnp.dot(root_left, gradient, preferred_element_type=jnp.float32).astype(jnp.bfloat16)
    raw_direction = jnp.dot(inner_rows, root_right, preferred_element_type=jnp.float32)
    grad_mean = jnp.mean(jnp.square(gradient.astype(jnp.float32)))
    graft_scale = live_flag * jnp.sqrt(grad_mean) / jnp.sqrt(jnp.mean(raw_direction * raw_direction) + EPSILON)
    return (raw_direction * graft_scale).astype(jnp.bfloat16)

def reference(grad_parts, live_counts):
    summed = lax.optimization_barrier(jnp.sum(grad_parts.astype(jnp.float32), axis=0)).astype(jnp.bfloat16)
    slot_ids = jnp.arange(NBLK, dtype=jnp.int32)
    live_flags = (slot_ids[None, :] < live_counts[:, None]).astype(jnp.float32)
    outputs = lax.map(refresh, (summed.reshape(TOWERS * NBLK, B, B), live_flags.reshape(TOWERS * NBLK)))
    return outputs.reshape(TOWERS, NBLK, B, B)
```

```python
import functools

import jax
import jax.numpy as jnp
from jax import lax
from jax.experimental import pallas as pl
from jax.experimental.pallas import tpu as pltpu
from jax.sharding import PartitionSpec as P

DAMPING = 0.25
EPSILON = 1e-06
MESH = pl.DeviceIdType.MESH
F32 = jnp.float32
BF16 = jnp.bfloat16
MEAN = 1.125
STRIPES = 4


def product(a, b, contract=((1,), (0,))):
    return lax.dot_general(a, b, (contract, ((), ())), preferred_element_type=F32)


def split(value):
    high = value.astype(BF16)
    return high, (value - high.astype(F32)).astype(BF16)


def refresh(
    counts, grad, ret, xret,
    own, peer, summed, arrived, chosen, gbuf, work, half, high1, low1, high2, low2,
    inner, rroot, outgoing,
    own_sem, pair_send, pair_recv, x_send, x_recv, z_send, z_recv, f_send, f_recv,
    r_send, r_recv, o_send, o_recv, y_send, y_recv, local_sem,
):
    owners = lax.axis_size("block")
    extra = owners // 2
    extent = gbuf.shape[0]
    rows = extent // owners
    part = rows // 2
    core = lax.axis_index("dp")
    place = lax.axis_index("block")
    tower = lax.axis_index("scen")
    other_tower = tower + 1 - 2 * lax.rem(tower, 2)
    sibling = {"dp": 1 - core}
    across = {"scen": other_tower}

    def aligned(index):
        return pl.multiple_of(index, part)

    groups = ((owners, extra), (0, extra), (extra, owners - extra))

    def own_copy(i):
        first, count = groups[i]
        return pltpu.make_async_copy(
            grad.at[pl.ds(first, count), pl.ds(aligned(core * part), part), :],
            own.at[pl.ds(first, count)],
            own_sem.at[i],
        )

    def pair_copy(i):
        first, count = groups[i]
        return pltpu.make_async_remote_copy(
            src_ref=grad.at[pl.ds(first, count), pl.ds(aligned((1 - core) * part), part), :],
            dst_ref=peer.at[pl.ds(first, count)],
            send_sem=pair_send.at[i],
            recv_sem=pair_recv.at[i],
            device_id=sibling,
            device_id_type=MESH,
        )

    def x_copy(k):
        return pltpu.make_async_remote_copy(
            src_ref=summed.at[owners + k],
            dst_ref=arrived.at[k],
            send_sem=x_send.at[k],
            recv_sem=x_recv.at[k],
            device_id=across,
            device_id_type=MESH,
        )

    def own_rows(index):
        return pl.ds(aligned(index * rows + core * part), part)

    def z_copy(owner, source, source_place):
        return pltpu.make_async_remote_copy(
            src_ref=source,
            dst_ref=gbuf.at[own_rows(source_place)],
            send_sem=z_send.at[owner],
            recv_sem=z_recv.at[source_place],
            device_id={"block": owner},
            device_id_type=MESH,
        )

    def f_copy(index):
        return pltpu.make_async_remote_copy(
            src_ref=gbuf.at[own_rows(index)],
            dst_ref=gbuf.at[own_rows(index)],
            send_sem=f_send.at[index],
            recv_sem=f_recv.at[index],
            device_id=sibling,
            device_id_type=MESH,
        )

    for i in range(3):
        own_copy(i).start()

    barrier = pltpu.get_barrier_semaphore()
    pl.semaphore_signal(barrier, inc=1, device_id=sibling, device_id_type=MESH)
    pl.semaphore_signal(barrier, inc=1, device_id=across, device_id_type=MESH)
    for step in range(1, owners):
        pl.semaphore_signal(
            barrier,
            inc=1,
            device_id={"block": lax.rem(place + step, owners)},
            device_id_type=MESH,
        )
    pl.semaphore_wait(barrier, owners + 1)

    for i in range(3):
        pair_copy(i).start()

    def add_pair(i):
        first, count = groups[i]
        own_copy(i).wait()
        pair_copy(i).wait_recv()
        for slot in range(first, first + count):
            summed[slot] = (own[slot].astype(F32) + peer[slot].astype(F32)).astype(BF16)

    def give(owner, source):
        @pl.when(place != owner)
        def _():
            z_copy(owner, source, place).start()

        @pl.when(place == owner)
        def _():
            gbuf[own_rows(owner), :] = source[...]
            f_copy(owner).start()

    add_pair(0)
    for k in range(extra):
        x_copy(k).start()
    add_pair(1)
    for k in range(extra):
        give(2 * k, summed.at[k])
    add_pair(2)
    own_live = counts[tower]
    other_live = counts[other_tower]
    fullest = own_live > extra
    is_fullest = jnp.broadcast_to(own_live, (part, extent)) > extra
    for k in range(extra):
        x_copy(k).wait_recv()
        chosen[k] = jnp.where(
            is_fullest, summed[extra + k].astype(F32), arrived[k].astype(F32)
        ).astype(BF16)
        give(2 * k + 1, chosen.at[k])

    for step in range(1, owners):
        source = lax.rem(place + step, owners)
        z_copy(place, chosen.at[0], source).wait_recv()
        f_copy(source).start()
    for index in range(owners):
        f_copy(index).wait_recv()

    square = jnp.zeros((1, 1), F32)
    tall = extent // STRIPES
    for i in range(STRIPES):
        values = gbuf[pl.ds(i * tall, tall), :].astype(F32)
        square += jnp.sum(values * values, axis=(0, 1), keepdims=True)
    mean = square / extent
    damping = DAMPING * mean + EPSILON
    rate = 0.25 / (2.0 * (mean + damping))

    def diagonal(i):
        row = lax.broadcasted_iota(jnp.int32, (tall, extent), 0) + i * tall
        column = lax.broadcasted_iota(jnp.int32, (tall, extent), 1)
        return row == column

    @pl.when(core == 0)
    def _():
        for i in range(STRIPES):
            work[pl.ds(i * tall, tall), :] = product(
                gbuf[pl.ds(i * tall, tall), :], gbuf[...], ((1,), (1,))
            )

    @pl.when(core == 1)
    def _():
        for i in range(STRIPES):
            work[pl.ds(i * tall, tall), :] = product(
                gbuf[:, pl.ds(i * tall, tall)], gbuf[...], ((0,), (0,))
            )

    for i in range(STRIPES):
        stripe = pl.ds(i * tall, tall)
        shift = jnp.where(diagonal(i), (1.25 - MEAN) - damping * rate, 0.0)
        error = shift - work[stripe, :] * rate
        work[stripe, :] = error
        high1[stripe, :], low1[stripe, :] = split(error)

    def precise(stripe, left_high, left_low, right_high, right_low):
        return (
            product(left_high[stripe, :], right_high[...])
            + product(left_high[stripe, :], right_low[...])
            + product(left_low[stripe, :], right_high[...])
        )

    for i in range(STRIPES):
        stripe = pl.ds(i * tall, tall)
        error = work[stripe, :]
        squared = precise(stripe, high1, low1, high1, low1) + (2 * MEAN) * error
        half[stripe, :] = squared
        high2[stripe, :], low2[stripe, :] = split(squared)
    for i in range(STRIPES):
        stripe = pl.ds(i * tall, tall)
        high1[stripe, :], low1[stripe, :] = split(5.0 * work[stripe, :] - 4.0 * half[stripe, :])

    mean2 = MEAN * MEAN
    mean4 = mean2 * mean2
    remain = 5.0 * MEAN - 4.0 * mean2

    def r_copy(i, buffer):
        return pltpu.make_async_remote_copy(
            src_ref=buffer.at[pl.ds(i * tall, tall)],
            dst_ref=buffer.at[pl.ds(i * tall, tall)],
            send_sem=r_send.at[i],
            recv_sem=r_recv.at[i],
            device_id=sibling,
            device_id_type=MESH,
        )

    for i in range(STRIPES):
        stripe = pl.ds(i * tall, tall)
        squared = half[stripe, :]
        fourth = precise(stripe, high2, low2, high2, low2) + (2 * mean2) * squared
        fourth_high, fourth_low = split(fourth)
        error = work[stripe, :]
        mapped = (
            product(fourth_high, high1[...])
            + product(fourth_high, low1[...])
            + product(fourth_low, high1[...])
            + mean4 * (5.0 * error - 4.0 * squared)
            + remain * fourth
        )
        root = (5.0 * error - mapped) * 0.25
        root += jnp.where(diagonal(i), (5.0 * MEAN - mean4 * remain) * 0.25, 0.0)
        rounded = root.astype(BF16)

        @pl.when(core == 0)
        def _():
            inner[stripe, :] = product(rounded, gbuf[...]).astype(BF16)
            r_copy(i, inner).start()

        @pl.when(core == 1)
        def _():
            rroot[stripe, :] = rounded
            r_copy(i, rroot).start()

    for i in range(STRIPES):
        @pl.when(core == 0)
        def _():
            r_copy(i, rroot).wait_recv()

        @pl.when(core == 1)
        def _():
            r_copy(i, inner).wait_recv()

    total = jnp.zeros((1, 1), F32)
    for i in range(STRIPES):
        stripe = pl.ds(i * tall, tall)
        raw = product(inner[stripe, :], rroot[...])
        work[stripe, :] = raw
        total += jnp.sum(raw * raw, axis=(0, 1), keepdims=True)

    spot = place // 2
    hosted = jnp.where(fullest, own_live > extra + spot, other_live > owners + spot)
    live = jnp.where(lax.rem(place, 2) == 0, own_live > spot, hosted)
    flag = jnp.where(live, 1.0, 0.0).astype(F32)
    entries = float(extent * extent)
    scale = flag * jnp.sqrt(square / entries) / jnp.sqrt(total / entries + EPSILON)

    def o_copy(target, source_place):
        return pltpu.make_async_remote_copy(
            src_ref=outgoing.at[target],
            dst_ref=ret.at[source_place],
            send_sem=o_send.at[target],
            recv_sem=o_recv.at[source_place],
            device_id={"block": target},
            device_id_type=MESH,
        )

    def y_copy(k):
        return pltpu.make_async_remote_copy(
            src_ref=ret.at[2 * k + 1],
            dst_ref=xret.at[k],
            send_sem=y_send.at[k],
            recv_sem=y_recv.at[k],
            device_id=across,
            device_id_type=MESH,
        )

    home = pltpu.make_async_copy(outgoing.at[place], ret.at[place], local_sem)
    for step in range(owners - 1, -1, -1):
        target = lax.rem(place + step, owners)
        outgoing[target] = (work[own_rows(target), :] * scale).astype(BF16)
        if step:
            o_copy(target, place).start()
        else:
            home.start()

    for owner in range(owners):
        @pl.when(place != owner)
        def _():
            o_copy(place, owner).wait_recv()

        @pl.when(place == owner)
        def _():
            home.wait()

        if owner % 2:
            y_copy(owner // 2).start()

    for i in range(3):
        pair_copy(i).wait_send()
    for k in range(extra):
        x_copy(k).wait_send()
    for owner in range(owners):
        f_copy(owner).wait_send()

        @pl.when(place != owner)
        def _():
            z_copy(owner, chosen.at[0], place).wait_send()
            o_copy(owner, place).wait_send()
    for i in range(STRIPES):
        r_copy(i, inner).wait_send()
    for k in range(extra):
        y_copy(k).wait()


def shards(grad_parts, live_counts):
    grad_shard = grad_parts[0, 0]
    owners = lax.axis_size("block")
    extra = owners // 2
    slots, rows, extent = grad_shard.shape
    part = rows // 2
    sent = owners + extra
    dma = pltpu.SemaphoreType.DMA
    wide = (extent, extent)
    ret, xret = pl.pallas_call(
        refresh,
        out_shape=(
            jax.ShapeDtypeStruct((owners, part, extent), BF16),
            jax.ShapeDtypeStruct((extra, part, extent), BF16),
        ),
        in_specs=[pl.BlockSpec(memory_space=pltpu.SMEM), pl.BlockSpec(memory_space=pl.ANY)],
        out_specs=[pl.BlockSpec(memory_space=pl.ANY)] * 2,
        scratch_shapes=[
            pltpu.VMEM((sent, part, extent), BF16),
            pltpu.VMEM((sent, part, extent), BF16),
            pltpu.VMEM((sent, part, extent), BF16),
            pltpu.VMEM((extra, part, extent), BF16),
            pltpu.VMEM((extra, part, extent), BF16),
            pltpu.VMEM(wide, BF16),
            pltpu.VMEM(wide, F32),
            pltpu.VMEM(wide, F32),
            pltpu.VMEM(wide, BF16),
            pltpu.VMEM(wide, BF16),
            pltpu.VMEM(wide, BF16),
            pltpu.VMEM(wide, BF16),
            pltpu.VMEM(wide, BF16),
            pltpu.VMEM(wide, BF16),
            pltpu.VMEM((owners, part, extent), BF16),
            dma((3,)), dma((3,)), dma((3,)),
            dma((extra,)), dma((extra,)),
            dma((owners,)), dma((owners,)),
            dma((owners,)), dma((owners,)),
            dma((STRIPES,)), dma((STRIPES,)),
            dma((owners,)), dma((owners,)),
            dma((extra,)), dma((extra,)),
            dma(()),
        ],
        compiler_params=pltpu.CompilerParams(
            collective_id=0, has_side_effects=True, vmem_limit_bytes=32 * 2**20
        ),
        name="refresh",
    )(live_counts, grad_shard)
    fullest = live_counts[lax.axis_index("scen")] > extra
    own_even = ret[0::2]
    zero = jnp.zeros((), BF16)
    own_odd = jnp.where(fullest, ret[1::2], zero)
    back = jnp.where(fullest, xret, zero)
    idle = jnp.zeros((slots - sent, part, extent), BF16)
    return jnp.concatenate([own_even, own_odd, back, idle], axis=0)[None]


def solution(mesh):
    in_specs = (P("dp", ("groups", "scen"), None, "block", None), P("groups"))
    out_specs = P(("groups", "scen"), None, ("block", "dp"), None)
    return jax.shard_map(shards, mesh=mesh, in_specs=in_specs, out_specs=out_specs, check_vma=False)
```

```python
import jax
import jax.numpy as jnp
from jax import lax
from jax.experimental import pallas as pl
from jax.experimental.pallas import tpu as pltpu
from jax.sharding import PartitionSpec as P

DAMPING = 0.25
EPSILON = 1e-06
MESH = pl.DeviceIdType.MESH
F32 = jnp.float32
BF16 = jnp.bfloat16
MEAN = 1.125
STRIPES = 1


def product(a, b, contract=((1,), (0,))):
    return lax.dot_general(a, b, (contract, ((), ())), preferred_element_type=F32)


def split(value):
    high = value.astype(BF16)
    return high, (value - high.astype(F32)).astype(BF16)


def refresh(
    counts, grad, ret, xret, mask,
    own, peer, summed, arrived, chosen, gbuf, work, half, high1, low1, high2, low2,
    inner, rroot, outgoing, flags,
    own_sem, pair_send, pair_recv, x_send, x_recv, z_send, z_recv, f_send, f_recv,
    r_send, r_recv, o_send, o_recv, y_send, y_recv, local_sem, mask_sem,
):
    owners = lax.axis_size("block")
    extra = owners // 2
    extent = gbuf.shape[0]
    rows = extent // owners
    part = rows // 2
    core = lax.axis_index("dp")
    place = lax.axis_index("block")
    tower = lax.axis_index("scen")
    other_tower = tower + 1 - 2 * lax.rem(tower, 2)
    sibling = {"dp": 1 - core}
    across = {"scen": other_tower}

    def aligned(index):
        return pl.multiple_of(index, part)

    groups = ((owners, extra), (0, extra), (extra, owners - extra))

    def own_copy(i):
        first, count = groups[i]
        return pltpu.make_async_copy(
            grad.at[pl.ds(first, count), pl.ds(aligned(core * part), part), :],
            own.at[pl.ds(first, count)],
            own_sem.at[i],
        )

    def pair_copy(i):
        first, count = groups[i]
        return pltpu.make_async_remote_copy(
            src_ref=grad.at[pl.ds(first, count), pl.ds(aligned((1 - core) * part), part), :],
            dst_ref=peer.at[pl.ds(first, count)],
            send_sem=pair_send.at[i],
            recv_sem=pair_recv.at[i],
            device_id=sibling,
            device_id_type=MESH,
        )

    def x_copy(k):
        return pltpu.make_async_remote_copy(
            src_ref=summed.at[owners + k],
            dst_ref=arrived.at[k],
            send_sem=x_send.at[k],
            recv_sem=x_recv.at[k],
            device_id=across,
            device_id_type=MESH,
        )

    def own_rows(index):
        return pl.ds(aligned(index * rows + core * part), part)

    def z_copy(owner, source, source_place):
        return pltpu.make_async_remote_copy(
            src_ref=source,
            dst_ref=gbuf.at[own_rows(source_place)],
            send_sem=z_send.at[owner],
            recv_sem=z_recv.at[source_place],
            device_id={"block": owner},
            device_id_type=MESH,
        )

    def f_copy(index):
        return pltpu.make_async_remote_copy(
            src_ref=gbuf.at[own_rows(index)],
            dst_ref=gbuf.at[own_rows(index)],
            send_sem=f_send.at[index],
            recv_sem=f_recv.at[index],
            device_id=sibling,
            device_id_type=MESH,
        )

    for i in range(3):
        own_copy(i).start()

    barrier = pltpu.get_barrier_semaphore()
    pl.semaphore_signal(barrier, inc=1, device_id=sibling, device_id_type=MESH)
    pl.semaphore_signal(barrier, inc=1, device_id=across, device_id_type=MESH)
    for step in range(1, owners):
        pl.semaphore_signal(
            barrier,
            inc=1,
            device_id={"block": lax.rem(place + step, owners)},
            device_id_type=MESH,
        )
    pl.semaphore_wait(barrier, owners + 1)

    for i in range(3):
        pair_copy(i).start()

    def add_pair(i):
        first, count = groups[i]
        own_copy(i).wait()
        pair_copy(i).wait_recv()
        for slot in range(first, first + count):
            summed[slot] = (own[slot].astype(F32) + peer[slot].astype(F32)).astype(BF16)

    def give(owner, source):
        @pl.when(place != owner)
        def _():
            z_copy(owner, source, place).start()

        @pl.when(place == owner)
        def _():
            gbuf[own_rows(owner), :] = source[...]
            f_copy(owner).start()

    add_pair(0)
    for k in range(extra):
        x_copy(k).start()
    add_pair(1)
    for k in range(extra):
        give(2 * k, summed.at[k])
    add_pair(2)
    own_live = counts[tower]
    other_live = counts[other_tower]
    fullest = own_live > extra
    flags[...] = jnp.where(jnp.broadcast_to(own_live, (1, extent)) > extra, 1.0, 0.0)
    mask_copy = pltpu.make_async_copy(flags, mask, mask_sem)
    mask_copy.start()
    is_fullest = jnp.broadcast_to(own_live, (part, extent)) > extra
    for k in range(extra):
        x_copy(k).wait_recv()
        chosen[k] = jnp.where(
            is_fullest, summed[extra + k].astype(F32), arrived[k].astype(F32)
        ).astype(BF16)
        give(2 * k + 1, chosen.at[k])

    for step in range(1, owners):
        source = lax.rem(place + step, owners)
        z_copy(place, chosen.at[0], source).wait_recv()
        f_copy(source).start()
    for index in range(owners):
        f_copy(index).wait_recv()

    square = jnp.zeros((1, 1), F32)
    tall = extent // STRIPES
    for i in range(STRIPES):
        values = gbuf[pl.ds(i * tall, tall), :].astype(F32)
        square += jnp.sum(values * values, axis=(0, 1), keepdims=True)
    mean = square / extent
    damping = DAMPING * mean + EPSILON
    rate = 0.25 / (2.0 * (mean + damping))

    def diagonal(i):
        row = lax.broadcasted_iota(jnp.int32, (tall, extent), 0) + i * tall
        column = lax.broadcasted_iota(jnp.int32, (tall, extent), 1)
        return row == column

    @pl.when(core == 0)
    def _():
        for i in range(STRIPES):
            work[pl.ds(i * tall, tall), :] = product(
                gbuf[pl.ds(i * tall, tall), :], gbuf[...], ((1,), (1,))
            )

    @pl.when(core == 1)
    def _():
        for i in range(STRIPES):
            work[pl.ds(i * tall, tall), :] = product(
                gbuf[:, pl.ds(i * tall, tall)], gbuf[...], ((0,), (0,))
            )

    for i in range(STRIPES):
        stripe = pl.ds(i * tall, tall)
        shift = jnp.where(diagonal(i), (1.25 - MEAN) - damping * rate, 0.0)
        error = shift - work[stripe, :] * rate
        work[stripe, :] = error
        high1[stripe, :], low1[stripe, :] = split(error)

    def precise(stripe, left_high, left_low, right_high, right_low):
        return (
            product(left_high[stripe, :], right_high[...])
            + product(left_high[stripe, :], right_low[...])
            + product(left_low[stripe, :], right_high[...])
        )

    for i in range(STRIPES):
        stripe = pl.ds(i * tall, tall)
        error = work[stripe, :]
        squared = precise(stripe, high1, low1, high1, low1) + (2 * MEAN) * error
        half[stripe, :] = squared
        high2[stripe, :], low2[stripe, :] = split(squared)
    for i in range(STRIPES):
        stripe = pl.ds(i * tall, tall)
        high1[stripe, :], low1[stripe, :] = split(5.0 * work[stripe, :] - 4.0 * half[stripe, :])

    mean2 = MEAN * MEAN
    mean4 = mean2 * mean2
    remain = 5.0 * MEAN - 4.0 * mean2

    def r_copy(i, buffer):
        return pltpu.make_async_remote_copy(
            src_ref=buffer.at[pl.ds(i * tall, tall)],
            dst_ref=buffer.at[pl.ds(i * tall, tall)],
            send_sem=r_send.at[i],
            recv_sem=r_recv.at[i],
            device_id=sibling,
            device_id_type=MESH,
        )

    for i in range(STRIPES):
        stripe = pl.ds(i * tall, tall)
        squared = half[stripe, :]
        fourth = precise(stripe, high2, low2, high2, low2) + (2 * mean2) * squared
        fourth_high, fourth_low = split(fourth)
        error = work[stripe, :]
        mapped = (
            product(fourth_high, high1[...])
            + product(fourth_high, low1[...])
            + product(fourth_low, high1[...])
            + mean4 * (5.0 * error - 4.0 * squared)
            + remain * fourth
        )
        root = (5.0 * error - mapped) * 0.25
        root += jnp.where(diagonal(i), (5.0 * MEAN - mean4 * remain) * 0.25, 0.0)
        rounded = root.astype(BF16)

        @pl.when(core == 0)
        def _():
            inner[stripe, :] = product(rounded, gbuf[...]).astype(BF16)
            r_copy(i, inner).start()

        @pl.when(core == 1)
        def _():
            rroot[stripe, :] = rounded
            r_copy(i, rroot).start()

    for i in range(STRIPES):
        @pl.when(core == 0)
        def _():
            r_copy(i, rroot).wait_recv()

        @pl.when(core == 1)
        def _():
            r_copy(i, inner).wait_recv()

    total = jnp.zeros((1, 1), F32)
    for i in range(STRIPES):
        stripe = pl.ds(i * tall, tall)
        raw = product(inner[stripe, :], rroot[...])
        work[stripe, :] = raw
        total += jnp.sum(raw * raw, axis=(0, 1), keepdims=True)

    spot = place // 2
    hosted = jnp.where(fullest, own_live > extra + spot, other_live > owners + spot)
    live = jnp.where(lax.rem(place, 2) == 0, own_live > spot, hosted)
    flag = jnp.where(live, 1.0, 0.0).astype(F32)
    entries = float(extent * extent)
    scale = flag * jnp.sqrt(square / entries) / jnp.sqrt(total / entries + EPSILON)

    def o_copy(target, source_place):
        return pltpu.make_async_remote_copy(
            src_ref=outgoing.at[target],
            dst_ref=ret.at[source_place],
            send_sem=o_send.at[target],
            recv_sem=o_recv.at[source_place],
            device_id={"block": target},
            device_id_type=MESH,
        )

    def y_copy(k):
        return pltpu.make_async_remote_copy(
            src_ref=ret.at[2 * k + 1],
            dst_ref=xret.at[k],
            send_sem=y_send.at[k],
            recv_sem=y_recv.at[k],
            device_id=across,
            device_id_type=MESH,
        )

    home = pltpu.make_async_copy(outgoing.at[place], ret.at[place], local_sem)
    for step in range(owners):
        target = lax.rem(place + step, owners)
        outgoing[target] = (work[own_rows(target), :] * scale).astype(BF16)
        if step:
            o_copy(target, place).start()
        else:
            home.start()

    for owner in range(owners):
        @pl.when(place != owner)
        def _():
            o_copy(place, owner).wait_recv()

        @pl.when(place == owner)
        def _():
            home.wait()

        if owner % 2:
            y_copy(owner // 2).start()

    mask_copy.wait()
    for i in range(3):
        pair_copy(i).wait_send()
    for k in range(extra):
        x_copy(k).wait_send()
    for owner in range(owners):
        f_copy(owner).wait_send()

        @pl.when(place != owner)
        def _():
            z_copy(owner, chosen.at[0], place).wait_send()
            o_copy(owner, place).wait_send()
    for i in range(STRIPES):
        r_copy(i, inner).wait_send()
    for k in range(extra):
        y_copy(k).wait()


def shards(grad_parts, live_counts):
    grad_shard = grad_parts[0, 0]
    owners = lax.axis_size("block")
    extra = owners // 2
    slots, rows, extent = grad_shard.shape
    part = rows // 2
    sent = owners + extra
    dma = pltpu.SemaphoreType.DMA
    wide = (extent, extent)
    ret, xret, mask = pl.pallas_call(
        refresh,
        out_shape=(
            jax.ShapeDtypeStruct((owners, part, extent), BF16),
            jax.ShapeDtypeStruct((extra, part, extent), BF16),
            jax.ShapeDtypeStruct((1, extent), F32),
        ),
        in_specs=[pl.BlockSpec(memory_space=pltpu.SMEM), pl.BlockSpec(memory_space=pl.ANY)],
        out_specs=[pl.BlockSpec(memory_space=pl.ANY)] * 3,
        scratch_shapes=[
            pltpu.VMEM((sent, part, extent), BF16),
            pltpu.VMEM((sent, part, extent), BF16),
            pltpu.VMEM((sent, part, extent), BF16),
            pltpu.VMEM((extra, part, extent), BF16),
            pltpu.VMEM((extra, part, extent), BF16),
            pltpu.VMEM(wide, BF16),
            pltpu.VMEM(wide, F32),
            pltpu.VMEM(wide, F32),
            pltpu.VMEM(wide, BF16),
            pltpu.VMEM(wide, BF16),
            pltpu.VMEM(wide, BF16),
            pltpu.VMEM(wide, BF16),
            pltpu.VMEM(wide, BF16),
            pltpu.VMEM(wide, BF16),
            pltpu.VMEM((owners, part, extent), BF16),
            pltpu.VMEM((1, extent), F32),
            dma((3,)), dma((3,)), dma((3,)),
            dma((extra,)), dma((extra,)),
            dma((owners,)), dma((owners,)),
            dma((owners,)), dma((owners,)),
            dma((STRIPES,)), dma((STRIPES,)),
            dma((owners,)), dma((owners,)),
            dma((extra,)), dma((extra,)),
            dma(()), dma(()),
        ],
        compiler_params=pltpu.CompilerParams(
            collective_id=0, has_side_effects=True, vmem_limit_bytes=32 * 2**20
        ),
        name="refresh",
    )(live_counts, grad_shard)
    fullest = mask[None] > 0.5
    own_even = ret[0::2]
    zero = jnp.zeros((), BF16)
    own_odd = jnp.where(fullest, ret[1::2], zero)
    back = jnp.where(fullest, xret, zero)
    idle = jnp.zeros((slots - sent, part, extent), BF16)
    return jnp.concatenate([own_even, own_odd, back, idle], axis=0)[None]


def solution(mesh):
    in_specs = (P("dp", ("groups", "scen"), None, "block", None), P("groups"))
    out_specs = P(("groups", "scen"), None, ("block", "dp"), None)
    return jax.shard_map(shards, mesh=mesh, in_specs=in_specs, out_specs=out_specs, check_vma=False)
```

```python
import jax
import jax.numpy as jnp
from jax import lax
from jax.experimental import pallas as pl
from jax.experimental.pallas import tpu as pltpu
from jax.sharding import PartitionSpec as P

DAMPING = 0.25
EPSILON = 1e-06
MESH = pl.DeviceIdType.MESH
F32 = jnp.float32
BF16 = jnp.bfloat16
MEAN = 1.125
STRIPES = 1


def product(a, b, contract=((1,), (0,))):
    return lax.dot_general(a, b, (contract, ((), ())), preferred_element_type=F32)


def split(value):
    high = value.astype(BF16)
    return high, (value - high.astype(F32)).astype(BF16)


def refresh(
    counts, grad, ret, xret, mask,
    own, peer, summed, arrived, chosen, gbuf, work, half, high1, low1, high2, low2,
    inner, rroot, outgoing, flags,
    own_sem, pair_send, pair_recv, x_send, x_recv, z_send, z_recv, f_send, f_recv,
    r_send, r_recv, o_send, o_recv, y_send, y_recv, local_sem, mask_sem,
):
    owners = lax.axis_size("block")
    extra = owners // 2
    extent = gbuf.shape[0]
    rows = extent // owners
    part = rows // 2
    core = lax.axis_index("dp")
    place = lax.axis_index("block")
    tower = lax.axis_index("scen")
    other_tower = tower + 1 - 2 * lax.rem(tower, 2)
    sibling = {"dp": 1 - core}
    across = {"scen": other_tower}

    def aligned(index):
        return pl.multiple_of(index, part)

    groups = ((owners, extra), (0, extra), (extra, owners - extra))

    def own_copy(i):
        first, count = groups[i]
        return pltpu.make_async_copy(
            grad.at[pl.ds(first, count), pl.ds(aligned(core * part), part), :],
            own.at[pl.ds(first, count)],
            own_sem.at[i],
        )

    def pair_copy(i):
        first, count = groups[i]
        return pltpu.make_async_remote_copy(
            src_ref=grad.at[pl.ds(first, count), pl.ds(aligned((1 - core) * part), part), :],
            dst_ref=peer.at[pl.ds(first, count)],
            send_sem=pair_send.at[i],
            recv_sem=pair_recv.at[i],
            device_id=sibling,
            device_id_type=MESH,
        )

    def x_copy(k):
        return pltpu.make_async_remote_copy(
            src_ref=summed.at[owners + k],
            dst_ref=arrived.at[k],
            send_sem=x_send.at[k],
            recv_sem=x_recv.at[k],
            device_id=across,
            device_id_type=MESH,
        )

    def own_rows(index):
        return pl.ds(aligned(index * rows + core * part), part)

    def z_copy(owner, source, source_place):
        return pltpu.make_async_remote_copy(
            src_ref=source,
            dst_ref=gbuf.at[own_rows(source_place)],
            send_sem=z_send.at[owner],
            recv_sem=z_recv.at[source_place],
            device_id={"block": owner},
            device_id_type=MESH,
        )

    def f_copy(index):
        return pltpu.make_async_remote_copy(
            src_ref=gbuf.at[own_rows(index)],
            dst_ref=gbuf.at[own_rows(index)],
            send_sem=f_send.at[index],
            recv_sem=f_recv.at[index],
            device_id=sibling,
            device_id_type=MESH,
        )

    for i in range(3):
        own_copy(i).start()

    barrier = pltpu.get_barrier_semaphore()
    pl.semaphore_signal(barrier, inc=1, device_id=sibling, device_id_type=MESH)
    pl.semaphore_signal(barrier, inc=1, device_id=across, device_id_type=MESH)
    for step in range(1, owners):
        pl.semaphore_signal(
            barrier,
            inc=1,
            device_id={"block": lax.rem(place + step, owners)},
            device_id_type=MESH,
        )
    pl.semaphore_wait(barrier, owners + 1)

    for i in range(3):
        pair_copy(i).start()

    def add_pair(i):
        first, count = groups[i]
        own_copy(i).wait()
        pair_copy(i).wait_recv()
        for slot in range(first, first + count):
            summed[slot] = (own[slot].astype(F32) + peer[slot].astype(F32)).astype(BF16)

    def give(owner, source):
        @pl.when(place != owner)
        def _():
            z_copy(owner, source, place).start()

        @pl.when(place == owner)
        def _():
            gbuf[own_rows(owner), :] = source[...]
            f_copy(owner).start()

    add_pair(0)
    for k in range(extra):
        x_copy(k).start()
    add_pair(1)
    for k in range(extra):
        give(2 * k, summed.at[k])
    add_pair(2)
    own_live = counts[tower]
    other_live = counts[other_tower]
    fullest = own_live > extra
    flags[...] = jnp.where(jnp.broadcast_to(own_live, (1, extent)) > extra, 1.0, 0.0)
    mask_copy = pltpu.make_async_copy(flags, mask, mask_sem)
    mask_copy.start()
    is_fullest = jnp.broadcast_to(own_live, (part, extent)) > extra
    for k in range(extra):
        x_copy(k).wait_recv()
        chosen[k] = jnp.where(
            is_fullest, summed[extra + k].astype(F32), arrived[k].astype(F32)
        ).astype(BF16)
        give(2 * k + 1, chosen.at[k])

    for step in range(1, owners):
        source = lax.rem(place + step, owners)
        z_copy(place, chosen.at[0], source).wait_recv()
        f_copy(source).start()
    for index in range(owners):
        f_copy(index).wait_recv()

    square = jnp.zeros((1, 1), F32)
    tall = extent // STRIPES
    for i in range(STRIPES):
        values = gbuf[pl.ds(i * tall, tall), :].astype(F32)
        square += jnp.sum(values * values, axis=(0, 1), keepdims=True)
    mean = square / extent
    damping = DAMPING * mean + EPSILON
    rate = 0.25 / (2.0 * (mean + damping))

    def diagonal(i):
        row = lax.broadcasted_iota(jnp.int32, (tall, extent), 0) + i * tall
        column = lax.broadcasted_iota(jnp.int32, (tall, extent), 1)
        return row == column

    @pl.when(core == 0)
    def _():
        for i in range(STRIPES):
            work[pl.ds(i * tall, tall), :] = product(
                gbuf[pl.ds(i * tall, tall), :], gbuf[...], ((1,), (1,))
            )

    @pl.when(core == 1)
    def _():
        for i in range(STRIPES):
            work[pl.ds(i * tall, tall), :] = product(
                gbuf[:, pl.ds(i * tall, tall)], gbuf[...], ((0,), (0,))
            )

    for i in range(STRIPES):
        stripe = pl.ds(i * tall, tall)
        shift = jnp.where(diagonal(i), (1.25 - MEAN) - damping * rate, 0.0)
        error = shift - work[stripe, :] * rate
        work[stripe, :] = error
        high1[stripe, :], low1[stripe, :] = split(error)

    def precise(stripe, left_high, left_low, right_high, right_low):
        return (
            product(left_high[stripe, :], right_high[...])
            + product(left_high[stripe, :], right_low[...])
            + product(left_low[stripe, :], right_high[...])
        )

    for i in range(STRIPES):
        stripe = pl.ds(i * tall, tall)
        error = work[stripe, :]
        squared = precise(stripe, high1, low1, high1, low1) + (2 * MEAN) * error
        half[stripe, :] = squared
        high2[stripe, :], low2[stripe, :] = split(squared)
    for i in range(STRIPES):
        stripe = pl.ds(i * tall, tall)
        high1[stripe, :], low1[stripe, :] = split(5.0 * work[stripe, :] - 4.0 * half[stripe, :])

    mean2 = MEAN * MEAN
    mean4 = mean2 * mean2
    remain = 5.0 * MEAN - 4.0 * mean2

    def r_copy(i, buffer):
        return pltpu.make_async_remote_copy(
            src_ref=buffer.at[pl.ds(i * tall, tall)],
            dst_ref=buffer.at[pl.ds(i * tall, tall)],
            send_sem=r_send.at[i],
            recv_sem=r_recv.at[i],
            device_id=sibling,
            device_id_type=MESH,
        )

    for i in range(STRIPES):
        stripe = pl.ds(i * tall, tall)
        squared = half[stripe, :]
        fourth = precise(stripe, high2, low2, high2, low2) + (2 * mean2) * squared
        fourth_high, fourth_low = split(fourth)
        error = work[stripe, :]
        mapped = (
            product(fourth_high, high1[...])
            + product(fourth_high, low1[...])
            + product(fourth_low, high1[...])
            + mean4 * (5.0 * error - 4.0 * squared)
            + remain * fourth
        )
        root = (5.0 * error - mapped) * 0.25
        root += jnp.where(diagonal(i), (5.0 * MEAN - mean4 * remain) * 0.25, 0.0)
        rounded = root.astype(BF16)

        @pl.when(core == 0)
        def _():
            inner[stripe, :] = product(rounded, gbuf[...]).astype(BF16)
            r_copy(i, inner).start()

        @pl.when(core == 1)
        def _():
            rroot[stripe, :] = rounded
            r_copy(i, rroot).start()

    for i in range(STRIPES):
        @pl.when(core == 0)
        def _():
            r_copy(i, rroot).wait_recv()

        @pl.when(core == 1)
        def _():
            r_copy(i, inner).wait_recv()

    total = jnp.zeros((1, 1), F32)
    for i in range(STRIPES):
        stripe = pl.ds(i * tall, tall)
        raw = product(inner[stripe, :], rroot[...])
        work[stripe, :] = raw
        total += jnp.sum(raw * raw, axis=(0, 1), keepdims=True)

    spot = place // 2
    hosted = jnp.where(fullest, own_live > extra + spot, other_live > owners + spot)
    live = jnp.where(lax.rem(place, 2) == 0, own_live > spot, hosted)
    flag = jnp.where(live, 1.0, 0.0).astype(F32)
    entries = float(extent * extent)
    scale = flag * jnp.sqrt(square / entries) / jnp.sqrt(total / entries + EPSILON)

    def o_copy(target, source_place):
        return pltpu.make_async_remote_copy(
            src_ref=outgoing.at[target],
            dst_ref=ret.at[source_place],
            send_sem=o_send.at[target],
            recv_sem=o_recv.at[source_place],
            device_id={"block": target},
            device_id_type=MESH,
        )

    def y_copy(k):
        return pltpu.make_async_remote_copy(
            src_ref=ret.at[2 * k + 1],
            dst_ref=xret.at[k],
            send_sem=y_send.at[k],
            recv_sem=y_recv.at[k],
            device_id=across,
            device_id_type=MESH,
        )

    home = pltpu.make_async_copy(outgoing.at[place], ret.at[place], local_sem)
    for step in range(owners):
        target = lax.rem(place + step, owners)
        outgoing[target] = (work[own_rows(target), :] * scale).astype(BF16)
        if step:
            o_copy(target, place).start()
        else:
            home.start()

    for owner in range(owners):
        @pl.when(place != owner)
        def _():
            o_copy(place, owner).wait_recv()

        @pl.when(place == owner)
        def _():
            home.wait()

        if owner % 2:
            y_copy(owner // 2).start()

    mask_copy.wait()
    for i in range(3):
        pair_copy(i).wait_send()
    for k in range(extra):
        x_copy(k).wait_send()
    for owner in range(owners):
        f_copy(owner).wait_send()

        @pl.when(place != owner)
        def _():
            z_copy(owner, chosen.at[0], place).wait_send()
            o_copy(owner, place).wait_send()
    for i in range(STRIPES):
        r_copy(i, inner).wait_send()
    for k in range(extra):
        y_copy(k).wait()


def shards(grad_parts, live_counts):
    grad_shard = grad_parts[0, 0]
    owners = lax.axis_size("block")
    extra = owners // 2
    slots, rows, extent = grad_shard.shape
    part = rows // 2
    sent = owners + extra
    dma = pltpu.SemaphoreType.DMA
    wide = (extent, extent)
    ret, xret, mask = pl.pallas_call(
        refresh,
        out_shape=(
            jax.ShapeDtypeStruct((owners, part, extent), BF16),
            jax.ShapeDtypeStruct((extra, part, extent), BF16),
            jax.ShapeDtypeStruct((1, extent), F32),
        ),
        in_specs=[pl.BlockSpec(memory_space=pltpu.SMEM), pl.BlockSpec(memory_space=pl.ANY)],
        out_specs=[pl.BlockSpec(memory_space=pl.ANY)] * 3,
        scratch_shapes=[
            pltpu.VMEM((sent, part, extent), BF16),
            pltpu.VMEM((sent, part, extent), BF16),
            pltpu.VMEM((sent, part, extent), BF16),
            pltpu.VMEM((extra, part, extent), BF16),
            pltpu.VMEM((extra, part, extent), BF16),
            pltpu.VMEM(wide, BF16),
            pltpu.VMEM(wide, F32),
            pltpu.VMEM(wide, F32),
            pltpu.VMEM(wide, BF16),
            pltpu.VMEM(wide, BF16),
            pltpu.VMEM(wide, BF16),
            pltpu.VMEM(wide, BF16),
            pltpu.VMEM(wide, BF16),
            pltpu.VMEM(wide, BF16),
            pltpu.VMEM((owners, part, extent), BF16),
            pltpu.VMEM((1, extent), F32),
            dma((3,)), dma((3,)), dma((3,)),
            dma((extra,)), dma((extra,)),
            dma((owners,)), dma((owners,)),
            dma((owners,)), dma((owners,)),
            dma((STRIPES,)), dma((STRIPES,)),
            dma((owners,)), dma((owners,)),
            dma((extra,)), dma((extra,)),
            dma(()), dma(()),
        ],
        compiler_params=pltpu.CompilerParams(
            collective_id=0, has_side_effects=True, vmem_limit_bytes=53 * 2**20
        ),
        name="refresh",
    )(live_counts, grad_shard)
    fullest = mask[None] > 0.5
    own_even = ret[0::2]
    zero = jnp.zeros((), BF16)
    own_odd = jnp.where(fullest, ret[1::2], zero)
    back = jnp.where(fullest, xret, zero)
    idle = jnp.zeros((slots - sent, part, extent), BF16)
    return jnp.concatenate([own_even, own_odd, back, idle], axis=0)[None]


def solution(mesh):
    in_specs = (P("dp", ("groups", "scen"), None, "block", None), P("groups"))
    out_specs = P(("groups", "scen"), None, ("block", "dp"), None)
    return jax.shard_map(shards, mesh=mesh, in_specs=in_specs, out_specs=out_specs, check_vma=False)
```

```python
import jax
import jax.numpy as jnp
from jax import lax
from jax.experimental import pallas as pl
from jax.experimental.pallas import tpu as pltpu
from jax.sharding import PartitionSpec as P

DAMPING = 0.25
EPSILON = 1e-06
MESH = pl.DeviceIdType.MESH
F32 = jnp.float32
BF16 = jnp.bfloat16
MEAN = 1.125
STRIPES = 1


def product(a, b, contract=((1,), (0,))):
    return lax.dot_general(a, b, (contract, ((), ())), preferred_element_type=F32)


def split(value):
    high = value.astype(BF16)
    return high, (value - high.astype(F32)).astype(BF16)


def refresh(
    counts, grad, ret, xret, mask,
    own, peer, summed, arrived, chosen, gbuf, work, half, high1, low1, high2, low2,
    inner, rroot, outgoing, flags,
    own_sem, pair_send, pair_recv, x_send, x_recv, z_send, z_recv, f_send, f_recv,
    r_send, r_recv, o_send, o_recv, y_send, y_recv, local_sem, mask_sem,
):
    owners = lax.axis_size("block")
    extra = owners // 2
    extent = gbuf.shape[0]
    rows = extent // owners
    part = rows // 2
    core = lax.axis_index("dp")
    place = lax.axis_index("block")
    tower = lax.axis_index("scen")
    other_tower = tower + 1 - 2 * lax.rem(tower, 2)
    sibling = {"dp": 1 - core}
    across = {"scen": other_tower}

    def aligned(index):
        return pl.multiple_of(index, part)

    groups = ((owners, extra), (0, extra), (extra, owners - extra))

    def own_copy(i):
        first, count = groups[i]
        return pltpu.make_async_copy(
            grad.at[pl.ds(first, count), pl.ds(aligned(core * part), part), :],
            own.at[pl.ds(first, count)],
            own_sem.at[i],
        )

    def pair_copy(i):
        first, count = groups[i]
        return pltpu.make_async_remote_copy(
            src_ref=grad.at[pl.ds(first, count), pl.ds(aligned((1 - core) * part), part), :],
            dst_ref=peer.at[pl.ds(first, count)],
            send_sem=pair_send.at[i],
            recv_sem=pair_recv.at[i],
            device_id=sibling,
            device_id_type=MESH,
        )

    def x_copy(k):
        return pltpu.make_async_remote_copy(
            src_ref=summed.at[owners + k],
            dst_ref=arrived.at[k],
            send_sem=x_send.at[k],
            recv_sem=x_recv.at[k],
            device_id=across,
            device_id_type=MESH,
        )

    def own_rows(index):
        return pl.ds(aligned(index * rows + core * part), part)

    def z_copy(owner, source, source_place):
        return pltpu.make_async_remote_copy(
            src_ref=source,
            dst_ref=gbuf.at[own_rows(source_place)],
            send_sem=z_send.at[owner],
            recv_sem=z_recv.at[source_place],
            device_id={"block": owner},
            device_id_type=MESH,
        )

    def f_copy(index):
        return pltpu.make_async_remote_copy(
            src_ref=gbuf.at[own_rows(index)],
            dst_ref=gbuf.at[own_rows(index)],
            send_sem=f_send.at[index],
            recv_sem=f_recv.at[index],
            device_id=sibling,
            device_id_type=MESH,
        )

    for i in range(3):
        own_copy(i).start()

    barrier = pltpu.get_barrier_semaphore()
    pl.semaphore_signal(barrier, inc=1, device_id=sibling, device_id_type=MESH)
    pl.semaphore_signal(barrier, inc=1, device_id=across, device_id_type=MESH)
    for step in range(1, owners):
        pl.semaphore_signal(
            barrier,
            inc=1,
            device_id={"block": lax.rem(place + step, owners)},
            device_id_type=MESH,
        )
    pl.semaphore_wait(barrier, owners + 1)

    for i in range(3):
        pair_copy(i).start()

    def add_pair(i):
        first, count = groups[i]
        own_copy(i).wait()
        pair_copy(i).wait_recv()
        for slot in range(first, first + count):
            summed[slot] = (own[slot].astype(F32) + peer[slot].astype(F32)).astype(BF16)

    def give(owner, source):
        @pl.when(place != owner)
        def _():
            z_copy(owner, source, place).start()

        @pl.when(place == owner)
        def _():
            gbuf[own_rows(owner), :] = source[...]
            f_copy(owner).start()

    add_pair(0)
    for k in range(extra):
        x_copy(k).start()
    add_pair(1)
    for k in range(extra):
        give(2 * k, summed.at[k])
    add_pair(2)
    own_live = counts[tower]
    other_live = counts[other_tower]
    fullest = own_live > extra
    flags[...] = jnp.where(jnp.broadcast_to(own_live, (1, extent)) > extra, 1.0, 0.0)
    mask_copy = pltpu.make_async_copy(flags, mask, mask_sem)
    mask_copy.start()
    is_fullest = jnp.broadcast_to(own_live, (part, extent)) > extra
    for k in range(extra):
        x_copy(k).wait_recv()
        chosen[k] = jnp.where(
            is_fullest, summed[extra + k].astype(F32), arrived[k].astype(F32)
        ).astype(BF16)
        give(2 * k + 1, chosen.at[k])

    for step in range(1, owners):
        source = lax.rem(place + step, owners)
        z_copy(place, chosen.at[0], source).wait_recv()
        f_copy(source).start()
    for index in range(owners):
        f_copy(index).wait_recv()

    square = jnp.zeros((1, 1), F32)
    tall = extent // STRIPES
    for i in range(STRIPES):
        values = gbuf[pl.ds(i * tall, tall), :].astype(F32)
        square += jnp.sum(values * values, axis=(0, 1), keepdims=True)
    mean = square / extent
    damping = DAMPING * mean + EPSILON
    rate = 0.25 / (2.0 * (mean + damping))

    def diagonal(i):
        row = lax.broadcasted_iota(jnp.int32, (tall, extent), 0) + i * tall
        column = lax.broadcasted_iota(jnp.int32, (tall, extent), 1)
        return row == column

    @pl.when(core == 0)
    def _():
        for i in range(STRIPES):
            work[pl.ds(i * tall, tall), :] = product(
                gbuf[pl.ds(i * tall, tall), :], gbuf[...], ((1,), (1,))
            )

    @pl.when(core == 1)
    def _():
        for i in range(STRIPES):
            work[pl.ds(i * tall, tall), :] = product(
                gbuf[:, pl.ds(i * tall, tall)], gbuf[...], ((0,), (0,))
            )

    for i in range(STRIPES):
        stripe = pl.ds(i * tall, tall)
        shift = jnp.where(diagonal(i), (1.25 - MEAN) - damping * rate, 0.0)
        error = shift - work[stripe, :] * rate
        work[stripe, :] = error
        high1[stripe, :], low1[stripe, :] = split(error)

    def precise(stripe, high, low):
        cross = product(high[...], low[...])
        return product(high[...], high[...]) + (cross + cross.T)

    for i in range(STRIPES):
        stripe = pl.ds(i * tall, tall)
        error = work[stripe, :]
        squared = precise(stripe, high1, low1) + (2 * MEAN) * error
        half[stripe, :] = squared
        high2[stripe, :], low2[stripe, :] = split(squared)
        high1[stripe, :], low1[stripe, :] = split(5.0 * error - 4.0 * squared)

    mean2 = MEAN * MEAN
    mean4 = mean2 * mean2
    remain = 5.0 * MEAN - 4.0 * mean2

    def r_copy(i, buffer):
        return pltpu.make_async_remote_copy(
            src_ref=buffer.at[pl.ds(i * tall, tall)],
            dst_ref=buffer.at[pl.ds(i * tall, tall)],
            send_sem=r_send.at[i],
            recv_sem=r_recv.at[i],
            device_id=sibling,
            device_id_type=MESH,
        )

    for i in range(STRIPES):
        stripe = pl.ds(i * tall, tall)
        squared = half[stripe, :]
        fourth = precise(stripe, high2, low2) + (2 * mean2) * squared
        fourth_high, fourth_low = split(fourth)
        error = work[stripe, :]
        mapped = (
            product(fourth_high, high1[...])
            + product(fourth_high, low1[...])
            + product(fourth_low, high1[...])
            + mean4 * (5.0 * error - 4.0 * squared)
            + remain * fourth
        )
        root = (5.0 * error - mapped) * 0.25
        root += jnp.where(diagonal(i), (5.0 * MEAN - mean4 * remain) * 0.25, 0.0)
        rounded = root.astype(BF16)

        @pl.when(core == 0)
        def _():
            inner[stripe, :] = product(rounded, gbuf[...]).astype(BF16)
            r_copy(i, inner).start()

        @pl.when(core == 1)
        def _():
            rroot[stripe, :] = rounded
            r_copy(i, rroot).start()

    for i in range(STRIPES):
        @pl.when(core == 0)
        def _():
            r_copy(i, rroot).wait_recv()

        @pl.when(core == 1)
        def _():
            r_copy(i, inner).wait_recv()

    total = jnp.zeros((1, 1), F32)
    for i in range(STRIPES):
        stripe = pl.ds(i * tall, tall)
        raw = product(inner[stripe, :], rroot[...])
        work[stripe, :] = raw
        total += jnp.sum(raw * raw, axis=(0, 1), keepdims=True)

    spot = place // 2
    hosted = jnp.where(fullest, own_live > extra + spot, other_live > owners + spot)
    live = jnp.where(lax.rem(place, 2) == 0, own_live > spot, hosted)
    flag = jnp.where(live, 1.0, 0.0).astype(F32)
    entries = float(extent * extent)
    scale = flag * jnp.sqrt(square / entries) / jnp.sqrt(total / entries + EPSILON)

    def o_copy(target, source_place):
        return pltpu.make_async_remote_copy(
            src_ref=outgoing.at[target],
            dst_ref=ret.at[source_place],
            send_sem=o_send.at[target],
            recv_sem=o_recv.at[source_place],
            device_id={"block": target},
            device_id_type=MESH,
        )

    def y_copy(k):
        return pltpu.make_async_remote_copy(
            src_ref=ret.at[2 * k + 1],
            dst_ref=xret.at[k],
            send_sem=y_send.at[k],
            recv_sem=y_recv.at[k],
            device_id=across,
            device_id_type=MESH,
        )

    home = pltpu.make_async_copy(outgoing.at[place], ret.at[place], local_sem)
    for step in range(owners):
        target = lax.rem(place + step, owners)
        outgoing[target] = (work[own_rows(target), :] * scale).astype(BF16)
        if step:
            o_copy(target, place).start()
        else:
            home.start()

    for owner in range(owners):
        @pl.when(place != owner)
        def _():
            o_copy(place, owner).wait_recv()

        @pl.when(place == owner)
        def _():
            home.wait()

        if owner % 2:
            y_copy(owner // 2).start()

    mask_copy.wait()
    for i in range(3):
        pair_copy(i).wait_send()
    for k in range(extra):
        x_copy(k).wait_send()
    for owner in range(owners):
        f_copy(owner).wait_send()

        @pl.when(place != owner)
        def _():
            z_copy(owner, chosen.at[0], place).wait_send()
            o_copy(owner, place).wait_send()
    for i in range(STRIPES):
        r_copy(i, inner).wait_send()
    for k in range(extra):
        y_copy(k).wait()


def shards(grad_parts, live_counts):
    grad_shard = grad_parts[0, 0]
    owners = lax.axis_size("block")
    extra = owners // 2
    slots, rows, extent = grad_shard.shape
    part = rows // 2
    sent = owners + extra
    dma = pltpu.SemaphoreType.DMA
    wide = (extent, extent)
    ret, xret, mask = pl.pallas_call(
        refresh,
        out_shape=(
            jax.ShapeDtypeStruct((owners, part, extent), BF16),
            jax.ShapeDtypeStruct((extra, part, extent), BF16),
            jax.ShapeDtypeStruct((1, extent), F32),
        ),
        in_specs=[pl.BlockSpec(memory_space=pltpu.SMEM), pl.BlockSpec(memory_space=pl.ANY)],
        out_specs=[pl.BlockSpec(memory_space=pl.ANY)] * 3,
        scratch_shapes=[
            pltpu.VMEM((sent, part, extent), BF16),
            pltpu.VMEM((sent, part, extent), BF16),
            pltpu.VMEM((sent, part, extent), BF16),
            pltpu.VMEM((extra, part, extent), BF16),
            pltpu.VMEM((extra, part, extent), BF16),
            pltpu.VMEM(wide, BF16),
            pltpu.VMEM(wide, F32),
            pltpu.VMEM(wide, F32),
            pltpu.VMEM(wide, BF16),
            pltpu.VMEM(wide, BF16),
            pltpu.VMEM(wide, BF16),
            pltpu.VMEM(wide, BF16),
            pltpu.VMEM(wide, BF16),
            pltpu.VMEM(wide, BF16),
            pltpu.VMEM((owners, part, extent), BF16),
            pltpu.VMEM((1, extent), F32),
            dma((3,)), dma((3,)), dma((3,)),
            dma((extra,)), dma((extra,)),
            dma((owners,)), dma((owners,)),
            dma((owners,)), dma((owners,)),
            dma((STRIPES,)), dma((STRIPES,)),
            dma((owners,)), dma((owners,)),
            dma((extra,)), dma((extra,)),
            dma(()), dma(()),
        ],
        compiler_params=pltpu.CompilerParams(
            collective_id=0, has_side_effects=True, vmem_limit_bytes=53 * 2**20
        ),
        name="refresh",
    )(live_counts, grad_shard)
    fullest = mask[None] > 0.5
    own_even = ret[0::2]
    zero = jnp.zeros((), BF16)
    own_odd = jnp.where(fullest, ret[1::2], zero)
    back = jnp.where(fullest, xret, zero)
    idle = jnp.zeros((slots - sent, part, extent), BF16)
    return jnp.concatenate([own_even, own_odd, back, idle], axis=0)[None]


def solution(mesh):
    in_specs = (P("dp", ("groups", "scen"), None, "block", None), P("groups"))
    out_specs = P(("groups", "scen"), None, ("block", "dp"), None)
    return jax.shard_map(shards, mesh=mesh, in_specs=in_specs, out_specs=out_specs, check_vma=False)
```

```python
import jax
import jax.numpy as jnp
from jax import lax
from jax.experimental import pallas as pl
from jax.experimental.pallas import tpu as pltpu
from jax.sharding import PartitionSpec as P

DAMPING = 0.25
EPSILON = 1e-06
MESH = pl.DeviceIdType.MESH
F32 = jnp.float32
BF16 = jnp.bfloat16
MEAN = 1.125
STRIPES = 1


def product(a, b, contract=((1,), (0,))):
    return lax.dot_general(a, b, (contract, ((), ())), preferred_element_type=F32)


def split(value):
    high = value.astype(BF16)
    return high, (value - high.astype(F32)).astype(BF16)


def refresh(
    counts, grad, ret, xret, mask,
    own, peer, summed, arrived, chosen, gbuf, work, half, high1, low1, high2, low2,
    inner, rroot, outgoing, flags,
    own_sem, pair_send, pair_recv, x_send, x_recv, z_send, z_recv, f_send, f_recv,
    r_send, r_recv, o_send, o_recv, y_send, y_recv, local_sem, mask_sem,
):
    owners = lax.axis_size("block")
    extra = owners // 2
    extent = gbuf.shape[0]
    rows = extent // owners
    part = rows // 2
    core = lax.axis_index("dp")
    place = lax.axis_index("block")
    tower = lax.axis_index("scen")
    other_tower = tower + 1 - 2 * lax.rem(tower, 2)
    sibling = {"dp": 1 - core}
    across = {"scen": other_tower}

    def aligned(index):
        return pl.multiple_of(index, part)

    groups = ((owners, extra), (0, extra), (extra, owners - extra))

    def own_copy(i):
        first, count = groups[i]
        return pltpu.make_async_copy(
            grad.at[pl.ds(first, count), pl.ds(aligned(core * part), part), :],
            own.at[pl.ds(first, count)],
            own_sem.at[i],
        )

    def pair_copy(i):
        first, count = groups[i]
        return pltpu.make_async_remote_copy(
            src_ref=grad.at[pl.ds(first, count), pl.ds(aligned((1 - core) * part), part), :],
            dst_ref=peer.at[pl.ds(first, count)],
            send_sem=pair_send.at[i],
            recv_sem=pair_recv.at[i],
            device_id=sibling,
            device_id_type=MESH,
        )

    def x_copy(k):
        return pltpu.make_async_remote_copy(
            src_ref=summed.at[owners + k],
            dst_ref=arrived.at[k],
            send_sem=x_send.at[k],
            recv_sem=x_recv.at[k],
            device_id=across,
            device_id_type=MESH,
        )

    def own_rows(index):
        return pl.ds(aligned(index * rows + core * part), part)

    def z_copy(owner, source, source_place):
        return pltpu.make_async_remote_copy(
            src_ref=source,
            dst_ref=gbuf.at[own_rows(source_place)],
            send_sem=z_send.at[owner],
            recv_sem=z_recv.at[source_place],
            device_id={"block": owner},
            device_id_type=MESH,
        )

    def f_copy(index):
        return pltpu.make_async_remote_copy(
            src_ref=gbuf.at[own_rows(index)],
            dst_ref=gbuf.at[own_rows(index)],
            send_sem=f_send.at[index],
            recv_sem=f_recv.at[index],
            device_id=sibling,
            device_id_type=MESH,
        )

    for i in range(3):
        own_copy(i).start()

    barrier = pltpu.get_barrier_semaphore()
    pl.semaphore_signal(barrier, inc=1, device_id=sibling, device_id_type=MESH)
    pl.semaphore_signal(barrier, inc=1, device_id=across, device_id_type=MESH)
    for step in range(1, owners):
        pl.semaphore_signal(
            barrier,
            inc=1,
            device_id={"block": lax.rem(place + step, owners)},
            device_id_type=MESH,
        )
    pl.semaphore_wait(barrier, owners + 1)

    for i in range(3):
        pair_copy(i).start()

    def add_pair(i):
        first, count = groups[i]
        own_copy(i).wait()
        pair_copy(i).wait_recv()
        for slot in range(first, first + count):
            summed[slot] = (own[slot].astype(F32) + peer[slot].astype(F32)).astype(BF16)

    def give(owner, source):
        @pl.when(place != owner)
        def _():
            z_copy(owner, source, place).start()

        @pl.when(place == owner)
        def _():
            gbuf[own_rows(owner), :] = source[...]
            f_copy(owner).start()

    add_pair(0)
    for k in range(extra):
        x_copy(k).start()
    add_pair(1)
    for k in range(extra):
        give(2 * k, summed.at[k])
    add_pair(2)
    own_live = counts[tower]
    other_live = counts[other_tower]
    fullest = own_live > extra
    flags[...] = jnp.where(jnp.broadcast_to(own_live, (1, extent)) > extra, 1.0, 0.0)
    mask_copy = pltpu.make_async_copy(flags, mask, mask_sem)
    mask_copy.start()
    is_fullest = jnp.broadcast_to(own_live, (part, extent)) > extra
    for k in range(extra):
        x_copy(k).wait_recv()
        chosen[k] = jnp.where(
            is_fullest, summed[extra + k].astype(F32), arrived[k].astype(F32)
        ).astype(BF16)
        give(2 * k + 1, chosen.at[k])

    for step in range(1, owners):
        source = lax.rem(place + step, owners)
        z_copy(place, chosen.at[0], source).wait_recv()
        f_copy(source).start()
    square = jnp.zeros((1, extent), F32)
    for index in range(owners):
        values = gbuf[own_rows(index), :].astype(F32)
        square += jnp.sum(values * values, axis=0, keepdims=True)
    for index in range(owners):
        f_copy(index).wait_recv()
        values = gbuf[pl.ds(aligned(index * rows + (1 - core) * part), part), :].astype(F32)
        square += jnp.sum(values * values, axis=0, keepdims=True)
    square = jnp.sum(square, axis=1, keepdims=True)

    tall = extent // STRIPES
    mean = square / extent
    damping = DAMPING * mean + EPSILON
    rate = 0.25 / (2.0 * (mean + damping))

    def diagonal(i):
        row = lax.broadcasted_iota(jnp.int32, (tall, extent), 0) + i * tall
        column = lax.broadcasted_iota(jnp.int32, (tall, extent), 1)
        return row == column

    @pl.when(core == 0)
    def _():
        for i in range(STRIPES):
            work[pl.ds(i * tall, tall), :] = product(
                gbuf[pl.ds(i * tall, tall), :], gbuf[...], ((1,), (1,))
            )

    @pl.when(core == 1)
    def _():
        for i in range(STRIPES):
            work[pl.ds(i * tall, tall), :] = product(
                gbuf[:, pl.ds(i * tall, tall)], gbuf[...], ((0,), (0,))
            )

    for i in range(STRIPES):
        stripe = pl.ds(i * tall, tall)
        shift = jnp.where(diagonal(i), (1.25 - MEAN) - damping * rate, 0.0)
        error = shift - work[stripe, :] * rate
        work[stripe, :] = error
        high1[stripe, :], low1[stripe, :] = split(error)

    def precise(stripe, high, low):
        cross = product(high[...], low[...])
        return product(high[...], high[...]) + (cross + cross.T)

    for i in range(STRIPES):
        stripe = pl.ds(i * tall, tall)
        error = work[stripe, :]
        squared = precise(stripe, high1, low1) + (2 * MEAN) * error
        half[stripe, :] = squared
        high2[stripe, :], low2[stripe, :] = split(squared)
        high1[stripe, :], low1[stripe, :] = split(5.0 * error - 4.0 * squared)

    mean2 = MEAN * MEAN
    mean4 = mean2 * mean2
    remain = 5.0 * MEAN - 4.0 * mean2

    def r_copy(i, buffer):
        return pltpu.make_async_remote_copy(
            src_ref=buffer.at[pl.ds(i * tall, tall)],
            dst_ref=buffer.at[pl.ds(i * tall, tall)],
            send_sem=r_send.at[i],
            recv_sem=r_recv.at[i],
            device_id=sibling,
            device_id_type=MESH,
        )

    for i in range(STRIPES):
        stripe = pl.ds(i * tall, tall)
        squared = half[stripe, :]
        fourth = precise(stripe, high2, low2) + (2 * mean2) * squared
        fourth_high, fourth_low = split(fourth)
        error = work[stripe, :]
        mapped = (
            product(fourth_high, high1[...])
            + product(fourth_high, low1[...])
            + product(fourth_low, high1[...])
            + mean4 * (5.0 * error - 4.0 * squared)
            + remain * fourth
        )
        root = (5.0 * error - mapped) * 0.25
        root += jnp.where(diagonal(i), (5.0 * MEAN - mean4 * remain) * 0.25, 0.0)
        rounded = root.astype(BF16)

        @pl.when(core == 0)
        def _():
            inner[stripe, :] = product(rounded, gbuf[...]).astype(BF16)
            r_copy(i, inner).start()

        @pl.when(core == 1)
        def _():
            rroot[stripe, :] = rounded
            r_copy(i, rroot).start()

    for i in range(STRIPES):
        @pl.when(core == 0)
        def _():
            r_copy(i, rroot).wait_recv()

        @pl.when(core == 1)
        def _():
            r_copy(i, inner).wait_recv()

    total = jnp.zeros((1, 1), F32)
    for i in range(STRIPES):
        stripe = pl.ds(i * tall, tall)
        raw = product(inner[stripe, :], rroot[...])
        work[stripe, :] = raw
        total += jnp.sum(raw * raw, axis=(0, 1), keepdims=True)

    spot = place // 2
    hosted = jnp.where(fullest, own_live > extra + spot, other_live > owners + spot)
    live = jnp.where(lax.rem(place, 2) == 0, own_live > spot, hosted)
    flag = jnp.where(live, 1.0, 0.0).astype(F32)
    entries = float(extent * extent)
    scale = flag * jnp.sqrt(square / entries) / jnp.sqrt(total / entries + EPSILON)

    def o_copy(target, source_place):
        return pltpu.make_async_remote_copy(
            src_ref=outgoing.at[target],
            dst_ref=ret.at[source_place],
            send_sem=o_send.at[target],
            recv_sem=o_recv.at[source_place],
            device_id={"block": target},
            device_id_type=MESH,
        )

    def y_copy(k, source):
        return pltpu.make_async_remote_copy(
            src_ref=source,
            dst_ref=xret.at[k],
            send_sem=y_send.at[k],
            recv_sem=y_recv.at[k],
            device_id=across,
            device_id_type=MESH,
        )

    home = pltpu.make_async_copy(outgoing.at[place], ret.at[place], local_sem)
    for step in range(owners):
        target = lax.rem(place + step, owners)
        outgoing[target] = (work[own_rows(target), :] * scale).astype(BF16)
        if step:
            o_copy(target, place).start()
        else:
            home.start()

            @pl.when(lax.rem(place, 2) == 1)
            def _():
                y_copy(place // 2, outgoing.at[place]).start()

    for k in range(extra):
        @pl.when(place != 2 * k + 1)
        def _():
            o_copy(place, 2 * k + 1).wait_recv()
            y_copy(k, ret.at[2 * k + 1]).start()

    for k in range(extra):
        @pl.when(place != 2 * k)
        def _():
            o_copy(place, 2 * k).wait_recv()

    home.wait()
    mask_copy.wait()
    for i in range(3):
        pair_copy(i).wait_send()
    for k in range(extra):
        x_copy(k).wait_send()
    for owner in range(owners):
        f_copy(owner).wait_send()

        @pl.when(place != owner)
        def _():
            z_copy(owner, chosen.at[0], place).wait_send()
            o_copy(owner, place).wait_send()
    for i in range(STRIPES):
        r_copy(i, inner).wait_send()
    for k in range(extra):
        y_copy(k, ret.at[2 * k + 1]).wait()


def shards(grad_parts, live_counts):
    grad_shard = grad_parts[0, 0]
    owners = lax.axis_size("block")
    extra = owners // 2
    slots, rows, extent = grad_shard.shape
    part = rows // 2
    sent = owners + extra
    dma = pltpu.SemaphoreType.DMA
    wide = (extent, extent)
    ret, xret, mask = pl.pallas_call(
        refresh,
        out_shape=(
            jax.ShapeDtypeStruct((owners, part, extent), BF16),
            jax.ShapeDtypeStruct((extra, part, extent), BF16),
            jax.ShapeDtypeStruct((1, extent), F32),
        ),
        in_specs=[pl.BlockSpec(memory_space=pltpu.SMEM), pl.BlockSpec(memory_space=pl.ANY)],
        out_specs=[pl.BlockSpec(memory_space=pl.ANY)] * 3,
        scratch_shapes=[
            pltpu.VMEM((sent, part, extent), BF16),
            pltpu.VMEM((sent, part, extent), BF16),
            pltpu.VMEM((sent, part, extent), BF16),
            pltpu.VMEM((extra, part, extent), BF16),
            pltpu.VMEM((extra, part, extent), BF16),
            pltpu.VMEM(wide, BF16),
            pltpu.VMEM(wide, F32),
            pltpu.VMEM(wide, F32),
            pltpu.VMEM(wide, BF16),
            pltpu.VMEM(wide, BF16),
            pltpu.VMEM(wide, BF16),
            pltpu.VMEM(wide, BF16),
            pltpu.VMEM(wide, BF16),
            pltpu.VMEM(wide, BF16),
            pltpu.VMEM((owners, part, extent), BF16),
            pltpu.VMEM((1, extent), F32),
            dma((3,)), dma((3,)), dma((3,)),
            dma((extra,)), dma((extra,)),
            dma((owners,)), dma((owners,)),
            dma((owners,)), dma((owners,)),
            dma((STRIPES,)), dma((STRIPES,)),
            dma((owners,)), dma((owners,)),
            dma((extra,)), dma((extra,)),
            dma(()), dma(()),
        ],
        compiler_params=pltpu.CompilerParams(
            collective_id=0, has_side_effects=True, vmem_limit_bytes=53 * 2**20
        ),
        name="refresh",
    )(live_counts, grad_shard)
    fullest = mask[None] > 0.5
    own_even = ret[0::2]
    zero = jnp.zeros((), BF16)
    own_odd = jnp.where(fullest, ret[1::2], zero)
    back = jnp.where(fullest, xret, zero)
    idle = jnp.zeros((slots - sent, part, extent), BF16)
    return jnp.concatenate([own_even, own_odd, back, idle], axis=0)[None]


def solution(mesh):
    in_specs = (P("dp", ("groups", "scen"), None, "block", None), P("groups"))
    out_specs = P(("groups", "scen"), None, ("block", "dp"), None)
    return jax.shard_map(shards, mesh=mesh, in_specs=in_specs, out_specs=out_specs, check_vma=False)
```
